32 devices in a mesh: groups: 2 (over y), dom: 16 (over z, x, core).
Axes of the slice: x: 2, y: 2, z: 4, core: 2. Of those that a mesh axis runs over, the one named last changes fastest.
Arguments:
- features: bfloat16 [8192, 1024], P(('groups', 'dom')), parts along dimension 0, may hold values from -6 to 6
- cotangent: bfloat16 [8192, 1024], P(('groups', 'dom')), parts along dimension 0, may hold values from -6 to 6
- w_self: bfloat16 [1024, 1024], replicated, may hold values from -0.1875 to 0.1875
- w_neigh: bfloat16 [1024, 1024], replicated, may hold values from -0.1875 to 0.1875
- history: bfloat16 [16384, 1024], P(('groups', 'dom')), parts along dimension 0, may hold values from -6 to 6
- hist_scale: bfloat16 [16384], P(('groups', 'dom')), parts along dimension 0, may hold values from 0.29882812 to 3
- send_rows: int32 [32, 16, 4], P(('groups', 'dom')), parts along dimension 0, may hold values from 0 to 511
- recv_counts: int32 [32, 16], P(('groups', 'dom')), parts along dimension 0, may hold values from 1 to 4, as said below
- neighbours: int32 [8192, 16], P(('groups', 'dom')), parts along dimension 0, may hold values from 0 to 63, as said below
- tile_index: int32 [256, 2], P(('groups', 'dom')), parts along dimension 0, may hold values from 0 to 1
- tile_mask: int32 [256, 128, 128], P(('groups', 'dom')), parts along dimension 0, may hold values 0 or 1
Outputs:
- grad_x: bfloat16 [8192, 1024], P(('groups', 'dom')), parts along dimension 0
- grad_self: float32 [2048, 1024], P(('groups', 'dom')), parts along dimension 0
- grad_neigh: float32 [2048, 1024], P(('groups', 'dom')), parts along dimension 0
The draws below stay inside these ranges and needn't reach their ends.
There are 2 independent parts, one for each index of `groups`. The reference program is written for one: setup_inputs(seed, part) draws one part's arguments, and reference() takes and returns one part's arrays. A program takes and returns all parts, laid end to end along the dimension named above; an argument that names none is the same for every part. Nothing has to cross between parts.
Inputs may be any that keep to these rules, and one draw needn't show every extreme that they name: `recv_counts`: each partition has an owner that fills all 4 slots for it. neighbours[i, k] = p * 4 + c names slot c of owner p for the partition of node i; references with c at or past recv_counts of that pair are not edges; the first reference of each node is an edge.
All inputs are finite; a program needn't handle non-finite values. No bound on the sum of `tile_mask` on one device may be relied on, other than what follows from the above.
Results may differ from the reference program's by a relative error of at most 0.0051.
Values may be sent and summed in bfloat16 or wider, within the bound.
A program may use at most 64 MiB of HBM per device.

```python
import math
import jax
import jax.numpy as jnp
from jax import lax

D = 1024
ROWS = 256
HIST = 512
CAP = 4
KNB = 16
TILES = 8
BLOCK = 128
TOKENS = 4096
N_DOM = 16


def shared_counts(key):
    base = jax.random.fold_in(key, 11)
    counts = jax.random.randint(base, (N_DOM, N_DOM), 1, CAP + 1)
    full = jnp.arange(N_DOM)[None, :] == (jnp.arange(N_DOM)[:, None] + 1) % N_DOM
    return jnp.where(full, CAP, counts).astype(jnp.int32)


def draw_recv_counts(key, part):
    counts = shared_counts(key)
    return counts


def draw_neighbours(key, part):
    counts = shared_counts(key)
    key = jax.random.fold_in(key, 2)
    key_owner, key_slot, key_first = jax.random.split(key, 3)
    owner = jax.random.randint(key_owner, (TOKENS, KNB), 0, N_DOM)
    position = jax.random.randint(key_slot, (TOKENS, KNB), 0, CAP)
    partition = jnp.arange(TOKENS) // ROWS
    filled = counts[partition[:, None], owner]
    first = jax.random.randint(key_first, (TOKENS, KNB), 0, 1 << 20) % filled
    column = jnp.arange(KNB)[None, :]
    position = jnp.where(column == 0, first, position)
    return (owner * CAP + position).astype(jnp.int32)


def plant(drawn, key, low, high):
    place = [jax.random.randint(jax.random.fold_in(key, axis), (), 0, length) for axis, length in enumerate(drawn.shape)]
    longest = drawn.shape.index(max(drawn.shape))
    beside = place[:longest] + [(place[longest] + 1) % drawn.shape[longest]] + place[longest + 1:]
    return drawn.at[tuple(place)].set(low).at[tuple(beside)].set(high)


def raised(values, key, source, target, parts, factor):
    owner, partner = [(jnp.arange(values.shape[axis_at]) // (values.shape[axis_at] // parts)).reshape([-1 if axis == axis_at else 1 for axis in range(values.ndim)]) for axis_at in (source, target)]
    chosen = jax.random.permutation(key, parts)[partner]
    strong = (owner == chosen) | (owner == (partner + parts // 2) % parts)
    return jnp.where(strong, factor * values, values)


def block_levels(rng, dims, pieces, smallest, high):
    level = 1.0
    for dim, parts in pieces:
        draws = jax.random.uniform(jax.random.fold_in(jax.random.fold_in(rng, 6), dim), (parts,), jnp.float32, smallest / len(pieces), high / len(pieces))
        level = level * jnp.repeat(jnp.exp(draws), dims[dim] // parts).reshape((-1,) + (1,) * (len(dims) - 1 - dim))
    return level


def gaussian(stream_key, dims, width, most, cuts=(), kind=jnp.bfloat16):
    array = jax.random.normal(stream_key, dims, jnp.float32) * width
    if len(cuts) > 0:
        array = block_levels(stream_key, dims, cuts, -0.22, 0.18) * array
    return jnp.clip(array, min=-most, max=most).astype(kind)


def gaussian_with(own_key, shape, scale, limit, cuts, heavy, held_as=jnp.bfloat16):
    result = scale * jax.random.normal(own_key, shape, jnp.float32)
    if cuts:
        result = result * block_levels(own_key, shape, cuts, -0.22, 0.18)
    return jnp.clip(raised(result, jax.random.fold_in(own_key, 3), *heavy), -limit, limit).astype(held_as)


def setup_inputs(seed: int = 0, part: int = 0) -> dict:
    splits = jax.random.split(jax.random.key(seed), 12)
    part_keys = jax.random.split(jax.random.fold_in(splits[11], part), 12)
    return {
        "features": gaussian_with(part_keys[0], (TOKENS, D), 1.0, 6.0, ((0, 16),), (0, 1, 16, 2.0)),
        "cotangent": gaussian(part_keys[1], (TOKENS, D), 1.0, 6.0, ((0, 16),)),
        "w_self": gaussian(splits[2], (D, D), D ** -0.5, 0.1875),
        "w_neigh": gaussian(splits[3], (D, D), D ** -0.5, 0.1875),
        "history": gaussian(part_keys[4], (N_DOM * HIST, D), 1.0, 6.0, ((0, 16),)),
        "hist_scale": jnp.clip(jnp.exp(math.log(3.0) - 2.306499 * jax.random.uniform(part_keys[5], (N_DOM * HIST,), jnp.float32) ** block_levels(part_keys[5], (N_DOM * HIST,), ((0, 16),), -0.2, 0.2)), 0.29882812, 3.0).astype(jnp.bfloat16),
        "send_rows": plant(jax.random.randint(part_keys[6], (N_DOM, N_DOM, CAP), 0, HIST), jax.random.fold_in(part_keys[6], 1), 0, HIST - 1).astype(jnp.int32),
        "recv_counts": draw_recv_counts(jax.random.fold_in(jax.random.fold_in(splits[11], part), 71), part),
        "neighbours": draw_neighbours(jax.random.fold_in(jax.random.fold_in(splits[11], part), 71), part),
        "tile_index": plant(jax.random.randint(part_keys[9], (N_DOM * TILES, 2), 0, ROWS // BLOCK), jax.random.fold_in(part_keys[9], 1), 0, (ROWS // BLOCK) - 1).astype(jnp.int32),
        "tile_mask": plant((jax.random.randint(part_keys[10], (N_DOM * TILES, BLOCK, BLOCK), 0, 32) < 1).astype(jnp.int32), jax.random.fold_in(part_keys[10], 1), 0, 1),
    }


def partition_step(index, features, cotangent, w_self, w_neigh, history, hist_scale, send_rows, recv_counts, neighbours, tile_index, tile_mask):
    inputs = lax.dynamic_slice_in_dim(features, index * ROWS, ROWS, 0)
    upstream = lax.dynamic_slice_in_dim(cotangent, index * ROWS, ROWS, 0)
    refs = lax.dynamic_slice_in_dim(neighbours, index * ROWS, ROWS, 0)
    tile_ids = lax.dynamic_slice_in_dim(tile_index, index * TILES, TILES, 0)
    masks = lax.dynamic_slice_in_dim(tile_mask, index * TILES, TILES, 0).astype(jnp.bfloat16)
    picked = lax.dynamic_index_in_dim(send_rows, index, 1, False)
    source = (jnp.arange(N_DOM, dtype=jnp.int32)[:, None] * HIST + picked).reshape(-1)
    slot_rows = history[source]
    slot_scale = hist_scale[source].astype(jnp.float32)
    counts = lax.dynamic_index_in_dim(recv_counts, index, 0, False)
    owner = refs // CAP
    position = refs % CAP
    live = (position < counts[owner]).astype(jnp.float32)
    weight = live * slot_scale[refs]
    remote_sum = jnp.zeros((ROWS, D), jnp.float32)
    for column in range(KNB):
        remote_sum = remote_sum + weight[:, column, None] * slot_rows[refs[:, column]].astype(jnp.float32)
    local_sum = jnp.zeros((ROWS, D), jnp.float32)
    edges = jnp.zeros((ROWS,), jnp.float32)
    for tile_number in range(TILES):
        row_block = tile_ids[tile_number, 0] * BLOCK
        col_block = tile_ids[tile_number, 1] * BLOCK
        block = lax.dynamic_slice_in_dim(inputs, col_block, BLOCK, 0)
        product = jnp.dot(masks[tile_number], block, preferred_element_type=jnp.float32)
        old = lax.dynamic_slice_in_dim(local_sum, row_block, BLOCK, 0)
        local_sum = lax.dynamic_update_slice_in_dim(local_sum, old + product, row_block, 0)
        old_edges = lax.dynamic_slice_in_dim(edges, row_block, BLOCK, 0)
        edges = lax.dynamic_update_slice_in_dim(edges, old_edges + jnp.sum(masks[tile_number].astype(jnp.float32), axis=1), row_block, 0)
    degree = edges + jnp.sum(live, axis=1)
    agg = ((local_sum + remote_sum) / degree[:, None]).astype(jnp.bfloat16)
    pre = jnp.dot(inputs, w_self, preferred_element_type=jnp.float32) + jnp.dot(agg, w_neigh, preferred_element_type=jnp.float32)
    sigma = jax.nn.sigmoid(pre)
    grad_pre = (upstream.astype(jnp.float32) * sigma * (1.0 + pre * (1.0 - sigma))).astype(jnp.bfloat16)
    contract_rows = (((0,), (0,)), ((), ()))
    contract_cols = (((1,), (1,)), ((), ()))
    self_term = lax.dot_general(inputs, grad_pre, contract_rows, preferred_element_type=jnp.float32)
    neigh_term = lax.dot_general(agg, grad_pre, contract_rows, preferred_element_type=jnp.float32)
    back = lax.dot_general(grad_pre, w_neigh, contract_cols, preferred_element_type=jnp.float32)
    back_agg = (back / degree[:, None]).astype(jnp.bfloat16)
    grad_rows = lax.dot_general(grad_pre, w_self, contract_cols, preferred_element_type=jnp.float32)
    for tile_number in range(TILES):
        row_block = tile_ids[tile_number, 0] * BLOCK
        col_block = tile_ids[tile_number, 1] * BLOCK
        block = lax.dynamic_slice_in_dim(back_agg, row_block, BLOCK, 0)
        product = lax.dot_general(masks[tile_number], block, contract_rows, preferred_element_type=jnp.float32)
        old = lax.dynamic_slice_in_dim(grad_rows, col_block, BLOCK, 0)
        grad_rows = lax.dynamic_update_slice_in_dim(grad_rows, old + product, col_block, 0)
    return grad_rows.astype(jnp.bfloat16), self_term, neigh_term


def reference(features, cotangent, w_self, w_neigh, history, hist_scale, send_rows, recv_counts, neighbours, tile_index, tile_mask):
    def one_partition(carry, index):
        grad_rows, self_term, neigh_term = partition_step(index, features, cotangent, w_self, w_neigh, history, hist_scale, send_rows, recv_counts, neighbours, tile_index, tile_mask)
        return (carry[0] + self_term, carry[1] + neigh_term), grad_rows

    start_sums = (jnp.zeros((D, D), jnp.float32), jnp.zeros((D, D), jnp.float32))
    totals, grad_blocks = lax.scan(one_partition, start_sums, jnp.arange(N_DOM, dtype=jnp.int32))
    factor = float(TOKENS) ** -0.5
    grad_x = grad_blocks.reshape(TOKENS, D)
    return grad_x, totals[0] * factor, totals[1] * factor
```

```python
import functools

import jax
import jax.numpy as jnp
from jax import lax
from jax.experimental import pallas as pl
from jax.experimental.pallas import tpu as pltpu
from jax.sharding import PartitionSpec as P

MESH = pl.DeviceIdType.MESH
F32 = jnp.float32
BF16 = jnp.bfloat16
PLANE = 4
LANES = 128
PER_PEER = 16


def iota(shape, dim):
    return lax.broadcasted_iota(jnp.int32, shape, dim)


def dot(a, b):
    return jnp.dot(a, b, preferred_element_type=F32)


def dot_nt(a, b):
    return lax.dot_general(a, b, (((1,), (1,)), ((), ())), preferred_element_type=F32)


def dot_tn(a, b):
    return lax.dot_general(a, b, (((0,), (0,)), ((), ())), preferred_element_type=F32)


def step_kernel(
    n, subs, factor,
    hist_ref, scale_ref, send_ref, count_ref, nb_ref, index_ref, f_hbm, mask_hbm, ws_hbm, wn_hbm, ct_hbm,
    gx_ref, gs_ref, gn_ref,
    f_ref, mask_ref, ws_ref, wn_ref, ct_ref, load_sem,
    out_rows, got_rows, rows_send, rows_recv,
    adj, agg_ref, grad, g_out, g_in, g_send, g_recv,
    f_out, f_in, f_send, f_recv, a_out, a_in, a_send, a_recv,
    part, right_out, right_in, left_out, left_in, right_send, right_recv, left_send, left_recv,
    swap_out, swap_in, swap_send, swap_recv,
):
    me = lax.axis_index("dom")
    core = me % 2
    x = (me // 2) % 2
    z = me // PLANE
    planes = n // PLANE
    rows, width = f_hbm.shape
    tiles, block, _ = mask_hbm.shape
    refs = nb_ref.shape[1]
    cap = send_ref.shape[2]
    hist = hist_ref.shape[0]
    segs = PER_PEER // cap
    seg = width // segs
    wide = n * PER_PEER
    slots = n * cap
    half = width // 2
    sub = half // subs
    units = 2 * subs
    rblk = width // (2 * planes)

    loads = []
    for k, (src, dst) in enumerate(((f_hbm, f_ref), (mask_hbm, mask_ref), (ws_hbm, ws_ref), (wn_hbm, wn_ref), (ct_hbm, ct_ref))):
        load = pltpu.make_async_copy(src, dst, load_sem.at[k])
        load.start()
        loads.append(load)

    barrier = pltpu.get_barrier_semaphore()

    def greet(k, carry):
        pl.semaphore_signal(barrier, inc=1, device_id={"dom": (me + k) % n}, device_id_type=MESH)
        return carry

    lax.fori_loop(1, n, greet, 0)

    sent = send_ref[0]
    expand = jnp.where((iota((wide, n), 0) // PER_PEER) == iota((wide, n), 1), 1.0, 0.0).astype(BF16)
    low = (sent % 256).astype(F32).astype(BF16)
    high = (sent // 256).astype(F32).astype(BF16)
    spread = dot(expand, low) + 256.0 * dot(expand, high)
    pick = jnp.where(iota((wide, cap), 1) == iota((wide, cap), 0) % cap, spread, 0.0)
    pick = jnp.sum(pick, axis=1, keepdims=True).astype(jnp.int32)
    hot = jnp.where(iota((wide, hist), 1) == pick, scale_ref[...].astype(F32), 0.0)
    seg_of = (iota((wide, hist), 0) // cap) % segs
    packed = jnp.zeros((wide, seg), F32)
    for j in range(segs):
        packed += dot(jnp.where(seg_of == j, hot, 0.0).astype(BF16), hist_ref[:, j * seg:(j + 1) * seg])
    out_rows[...] = packed.astype(BF16).reshape(n, PER_PEER, seg)

    pl.semaphore_wait(barrier, n - 1)

    def row_copy(k, source, target):
        return pltpu.make_async_remote_copy(
            src_ref=out_rows.at[target], dst_ref=got_rows.at[source],
            send_sem=rows_send.at[k], recv_sem=rows_recv.at[k],
            device_id={"dom": target}, device_id_type=MESH)

    def send_rows(k, carry):
        row_copy(k, me, (me + k) % n).start()
        return carry

    lax.fori_loop(1, n, send_rows, 0)
    got_rows[pl.ds(me, 1)] = out_rows[pl.ds(me, 1)]

    sibling = me + 1 - 2 * core
    across = me + 2 - 4 * x
    diagonal = sibling + 2 - 4 * x

    def remote(src, dst, send, recv, target):
        return pltpu.make_async_remote_copy(
            src_ref=src, dst_ref=dst, send_sem=send, recv_sem=recv,
            device_id={"dom": target}, device_id_type=MESH)

    def factor_copies(out, into, send, recv):
        return (
            remote(out.at[:, 1 - x], into.at[1], send.at[1], recv.at[1], across),
            remote(out.at[:, x], into.at[0], send.at[0], recv.at[0], sibling),
            remote(into.at[1], into.at[2], send.at[2], recv.at[2], sibling),
        )

    loads[0].wait()
    for j in range(planes):
        f_out[j] = f_ref[:, j * 2 * rblk:(j + 1) * 2 * rblk].T.reshape(2, rblk, rows)
    f_copies = factor_copies(f_out, f_in, f_send, f_recv)
    f_copies[0].start()
    f_copies[1].start()

    loads[1].wait()
    blocks = rows // block
    degree = []
    for b in range(blocks):
        edges = jnp.zeros((block, 1), F32)
        for e in range(blocks):
            total = jnp.zeros((block, block), jnp.int32)
            for t in range(tiles):
                here = (index_ref[t, 0] == b).astype(jnp.int32) * (index_ref[t, 1] == e).astype(jnp.int32)
                total += here * mask_ref[t]
            total = total.astype(F32)
            edges += jnp.sum(total, axis=1, keepdims=True)
            adj[b * block:(b + 1) * block, e * block:(e + 1) * block] = total.astype(BF16)
        degree.append(edges)
    degree = jnp.concatenate(degree, axis=0)
    filled = jnp.broadcast_to(count_ref[...], (8, n)).astype(F32).astype(BF16)
    owner = jnp.where(iota((n, slots), 1) // cap == iota((n, slots), 0), 1.0, 0.0).astype(BF16)
    filled = dot(filled, owner)[0:1]
    live = jnp.where((iota((1, slots), 1) % cap).astype(F32) < filled, 1.0, 0.0)
    count = jnp.zeros((rows, slots), F32)
    for k in range(refs):
        count += jnp.where(nb_ref[:, k:k + 1] == iota((rows, slots), 1), live, 0.0)
    degree += jnp.sum(count, axis=1, keepdims=True)
    count = count.astype(BF16)
    ws_ready, wn_ready, ct_ready = loads[2:]
    slot_of = (iota((slots, wide), 1) // PER_PEER) * cap + iota((slots, wide), 1) % cap
    same = slot_of == iota((slots, wide), 0)
    spread_seg = (iota((slots, wide), 1) // cap) % segs
    spreads = []
    for j in range(segs):
        e_j = jnp.where(same & (spread_seg == j), 1.0, 0.0).astype(BF16)
        spreads.append(dot(count, e_j).astype(BF16))
    ws_ready.wait()
    wn_ready.wait()
    ct_ready.wait()

    def got(k, carry):
        row_copy(k, (me + n - k) % n, (me + k) % n).wait_recv()
        return carry

    lax.fori_loop(1, n, got, 0)
    rows_in = got_rows[...].reshape(wide, seg)
    for j in range(segs):
        columns = slice(j * seg, (j + 1) * seg)
        total = dot(adj[...], f_ref[:, columns]) + dot(spreads[j], rows_in)
        agg_ref[:, columns] = (total / degree).astype(BF16)

    f_copies[0].wait_recv()
    f_copies[2].start()

    for j in range(planes):
        a_out[j] = agg_ref[:, j * 2 * rblk:(j + 1) * 2 * rblk].T.reshape(2, rblk, rows)
    a_copies = factor_copies(a_out, a_in, a_send, a_recv)

    def g_copies(s):
        return (
            remote(g_out.at[core, s], g_in.at[1, s], g_send.at[1, s], g_recv.at[1, s], across),
            remote(g_out.at[1 - core, s], g_in.at[2, s], g_send.at[2, s], g_recv.at[2, s], diagonal),
            remote(g_out.at[1 - core, s], g_in.at[0, s], g_send.at[0, s], g_recv.at[0, s], sibling),
        )

    for s in range(subs):
        for h in range(2):
            columns = slice(h * half + s * sub, h * half + (s + 1) * sub)
            pre = dot(f_ref[...], ws_ref[:, columns]) + dot(agg_ref[...], wn_ref[:, columns])
            sigma = jax.nn.sigmoid(pre)
            value = (ct_ref[:, columns].astype(F32) * sigma * (1.0 + pre * (1.0 - sigma))).astype(BF16)
            g_out[h, s] = value
            grad[:, columns] = value
        for copy in g_copies(s):
            copy.start()
        if s == 0:
            a_copies[0].start()
            a_copies[1].start()

    back = (dot_nt(grad[...], wn_ref[...]) / degree).astype(BF16)
    gx_ref[...] = (dot_nt(grad[...], ws_ref[...]) + dot_tn(adj[...], back)).astype(BF16)

    def unit_of(m, s):
        return 2 * s + m

    last = planes - 1

    def right(u, k):
        return remote(right_out.at[u, k], right_in.at[u, k], right_send.at[u, k], right_recv.at[u, k], (me + PLANE) % n)

    def left(u, k):
        return remote(left_out.at[u, k], left_in.at[u, k], left_send.at[u, k], left_recv.at[u, k], (me + n - PLANE) % n)

    def along(u, inner, first, final, copy, out, into, order, beyond):
        for k in order:
            @pl.when(beyond(k))
            def _():
                @pl.when(first)
                def _():
                    out[u, k] = part[u, k].astype(BF16)

                @pl.when(jnp.logical_not(first))
                def _():
                    copy(u, k).wait_recv()
                    out[u, k] = (part[u, k] + into[u, k].astype(F32)).astype(BF16)

                copy(u, k).start()

            @pl.when((z == k) & jnp.logical_not(first))
            def _():
                copy(u, k).wait_recv()
                part[u, k] += into[u, k].astype(F32)

    for t in range(units + last):
        if t < units:
            s, m = t // 2, t % 2
            if m == 0:
                for copy in g_copies(s):
                    copy.wait_recv()
            if t == 0:
                f_copies[1].wait_recv()
                f_copies[2].wait_recv()
            if t == 1:
                a_copies[0].wait_recv()
                a_copies[2].start()
                a_copies[1].wait_recv()
                a_copies[2].wait_recv()
            out, into = ((f_out, f_in), (a_out, a_in))[m]
            total = dot(out[:, x].reshape(planes * rblk, rows), g_out[core, s])
            for k in range(3):
                total += dot(into[k].reshape(planes * rblk, rows), g_in[k, s])
            part[t] = total.reshape(planes, rblk, sub)

        @pl.when((t - z >= 0) & (t - z < units))
        def _():
            along(t - z, z, z == 0, None, right, right_out, right_in, range(last, 0, -1), lambda k: k > z)

        away = t - (last - z)

        @pl.when((away >= 0) & (away < units))
        def _():
            along(away, z, z == last, None, left, left_out, left_in, range(last), lambda k: k < z)

    mine = rblk // 2
    for u in range(units):
        swap_out[u] = part[u, z, pl.ds(pl.multiple_of((1 - core) * mine, mine), mine)] * factor
        remote(swap_out.at[u], swap_in.at[u], swap_send.at[u], swap_recv.at[u], sibling).start()
    for u in range(units):
        s, m = u // 2, u % 2
        out = (gs_ref, gn_ref)[m]
        out[:, pl.ds(pl.multiple_of(core * half + s * sub, LANES), sub)] = (
            part[u, z, pl.ds(pl.multiple_of(core * mine, mine), mine)] * factor)
    for u in range(units):
        s, m = u // 2, u % 2
        out = (gs_ref, gn_ref)[m]
        remote(swap_out.at[u], swap_in.at[u], swap_send.at[u], swap_recv.at[u], sibling).wait()
        out[:, pl.ds(pl.multiple_of((1 - core) * half + s * sub, LANES), sub)] = swap_in[u]

    def left_rows(k, carry):
        row_copy(k, me, (me + k) % n).wait_send()
        return carry

    lax.fori_loop(1, n, left_rows, 0)
    for copy in (*f_copies, *a_copies):
        copy.wait_send()
    for s in range(subs):
        for copy in g_copies(s):
            copy.wait_send()
    for u in range(units):
        for k in range(planes):
            @pl.when(k > z)
            def _():
                right(u, k).wait_send()

            @pl.when(k < z)
            def _():
                left(u, k).wait_send()


def fused(
    subs, features, cotangent, w_self, w_neigh, history, hist_scale, send_rows, recv_counts, neighbours, tile_index, tile_mask
):
    n = lax.axis_size("dom")
    rows, width = features.shape
    planes = n // PLANE
    cap = send_rows.shape[2]
    seg = width * cap // PER_PEER
    sub = width // 2 // subs
    units = 2 * subs
    rblk = width // (2 * planes)
    factor = float(n * rows) ** (-0.5)
    vmem = pl.BlockSpec(memory_space=pltpu.VMEM)
    smem = pl.BlockSpec(memory_space=pltpu.SMEM)
    anywhere = pl.BlockSpec(memory_space=pl.ANY)
    dma = pltpu.SemaphoreType.DMA
    V = pltpu.VMEM
    line = (units, planes, rblk, sub)
    scratch = [
        V(features.shape, BF16), V(tile_mask.shape, jnp.int32), V(w_self.shape, BF16), V(w_neigh.shape, BF16),
        V(cotangent.shape, BF16), dma((5,)),
        V((n, PER_PEER, seg), BF16), V((n, PER_PEER, seg), BF16), dma((n,)), dma((n,)),
        V((rows, rows), BF16), V((rows, width), BF16), V((rows, width), BF16),
        V((2, subs, rows, sub), BF16), V((3, subs, rows, sub), BF16), dma((3, subs)), dma((3, subs)),
        V((planes, 2, rblk, rows), BF16), V((3, planes, rblk, rows), BF16), dma((3,)), dma((3,)),
        V((planes, 2, rblk, rows), BF16), V((3, planes, rblk, rows), BF16), dma((3,)), dma((3,)),
        V(line, F32), V(line, BF16), V(line, BF16), V(line, BF16), V(line, BF16),
        dma(line[:2]), dma(line[:2]), dma(line[:2]), dma(line[:2]),
        V((units, rblk // 2, sub), F32), V((units, rblk // 2, sub), F32), dma((units,)), dma((units,)),
    ]
    return pl.pallas_call(
        functools.partial(step_kernel, n, subs, factor),
        out_shape=(
            jax.ShapeDtypeStruct((rows, width), BF16),
            jax.ShapeDtypeStruct((width // n, width), F32),
            jax.ShapeDtypeStruct((width // n, width), F32),
        ),
        in_specs=[vmem, vmem, vmem, vmem, vmem, smem] + [anywhere] * 5,
        out_specs=(vmem, vmem, vmem),
        scratch_shapes=scratch,
        compiler_params=pltpu.CompilerParams(
            collective_id=0, has_side_effects=True, vmem_limit_bytes=48 * 1024 * 1024),
    )(history, hist_scale.reshape(1, -1), send_rows, recv_counts, neighbours, tile_index,
      features, tile_mask, w_self, w_neigh, cotangent)


def tiles_forward(inputs, tile_index, masks, block_size):
    row_total, feature_width = inputs.shape
    tile_count = masks.shape[0]
    local_sum = jnp.zeros((row_total, feature_width), jnp.float32)
    edges = jnp.zeros((row_total,), jnp.float32)
    for tile_number in range(tile_count):
        row_block = tile_index[tile_number, 0] * block_size
        col_block = tile_index[tile_number, 1] * block_size
        block = lax.dynamic_slice_in_dim(inputs, col_block, block_size, 0)
        product = jnp.dot(masks[tile_number], block, preferred_element_type=jnp.float32)
        older = lax.dynamic_slice_in_dim(local_sum, row_block, block_size, 0)
        local_sum = lax.dynamic_update_slice_in_dim(local_sum, older + product, row_block, 0)
        older_edges = lax.dynamic_slice_in_dim(edges, row_block, block_size, 0)
        edges = lax.dynamic_update_slice_in_dim(
            edges,
            older_edges + jnp.sum(masks[tile_number].astype(jnp.float32), axis=1),
            row_block,
            0,
        )
    return (local_sum, edges)


def tiles_backward(grad_rows, back_agg, tile_index, masks, block_size):
    tile_count = masks.shape[0]
    contract_rows = (((0,), (0,)), ((), ()))
    for tile_number in range(tile_count):
        row_block = tile_index[tile_number, 0] * block_size
        col_block = tile_index[tile_number, 1] * block_size
        block = lax.dynamic_slice_in_dim(back_agg, row_block, block_size, 0)
        product = lax.dot_general(
            masks[tile_number], block, contract_rows, preferred_element_type=jnp.float32
        )
        older = lax.dynamic_slice_in_dim(grad_rows, col_block, block_size, 0)
        grad_rows = lax.dynamic_update_slice_in_dim(grad_rows, older + product, col_block, 0)
    return grad_rows


def plain_shards(
    features,
    cotangent,
    w_self,
    w_neigh,
    history,
    hist_scale,
    send_rows,
    recv_counts,
    neighbours,
    tile_index,
    tile_mask,
):
    row_total, feature_width = features.shape
    peer_count = lax.axis_size("dom")
    slot_cap = send_rows.shape[2]
    block_size = tile_mask.shape[1]
    picked = send_rows[0]
    out_rows = history[picked]
    out_scale = hist_scale[picked]
    got_rows, got_scale = (
        lax.all_to_all(out_rows, "dom", split_axis=0, concat_axis=0, tiled=True),
        lax.all_to_all(out_scale, "dom", split_axis=0, concat_axis=0, tiled=True),
    )
    slot_total = peer_count * slot_cap
    got_rows = got_rows.reshape(slot_total, feature_width)
    got_scale = got_scale.reshape(slot_total).astype(jnp.float32)
    masks = tile_mask.astype(jnp.bfloat16)
    local_sum, edges = tiles_forward(features, tile_index, masks, block_size)
    counts = recv_counts[0]
    owner = neighbours // slot_cap
    position = neighbours % slot_cap
    live = (position < counts[owner]).astype(jnp.float32)
    weight = live * got_scale[neighbours]
    row_ids = jnp.broadcast_to(jnp.arange(row_total, dtype=jnp.int32)[:, None], neighbours.shape)
    slot_weight = (
        jnp.zeros((row_total, slot_total), jnp.float32).at[row_ids, neighbours].add(weight)
    )
    remote_sum = jnp.dot(slot_weight, got_rows.astype(jnp.float32), precision=lax.Precision.HIGHEST)
    degree = edges + jnp.sum(live, axis=1)
    agg = ((local_sum + remote_sum) / degree[:, None]).astype(jnp.bfloat16)
    pre = jnp.dot(features, w_self, preferred_element_type=jnp.float32) + jnp.dot(
        agg, w_neigh, preferred_element_type=jnp.float32
    )
    sigma = jax.nn.sigmoid(pre)
    grad_pre = (cotangent.astype(jnp.float32) * sigma * (1.0 + pre * (1.0 - sigma))).astype(
        jnp.bfloat16
    )
    factor = float(peer_count * row_total) ** (-0.5)
    contract_rows = (((0,), (0,)), ((), ()))
    contract_cols = (((1,), (1,)), ((), ()))
    columns = features
    grad_self = lax.psum_scatter(
        lax.dot_general(columns, grad_pre, contract_rows, preferred_element_type=jnp.float32)
        * factor,
        "dom",
        scatter_dimension=0,
        tiled=True,
    )
    columns = agg
    grad_neigh = lax.psum_scatter(
        lax.dot_general(columns, grad_pre, contract_rows, preferred_element_type=jnp.float32)
        * factor,
        "dom",
        scatter_dimension=0,
        tiled=True,
    )
    back = lax.dot_general(grad_pre, w_neigh, contract_cols, preferred_element_type=jnp.float32)
    back_agg = (back / degree[:, None]).astype(jnp.bfloat16)
    grad_rows = lax.dot_general(grad_pre, w_self, contract_cols, preferred_element_type=jnp.float32)
    grad_rows = tiles_backward(grad_rows, back_agg, tile_index, masks, block_size)
    return (grad_rows.astype(jnp.bfloat16), grad_self, grad_neigh)


def shards(subs, *args):
    features, send_rows, tile_mask = args[0], args[6], args[10]
    n = lax.axis_size("dom")
    width = features.shape[1]
    cap = send_rows.shape[2]
    whole_blocks = n % PLANE == 0 and (2 * width) % (n * LANES) == 0
    if whole_blocks and PER_PEER % cap == 0 and features.shape[0] % LANES == 0:
        return fused(subs, *args)
    return plain_shards(*args)


def solution(mesh):
    return jax.shard_map(
        functools.partial(shards, 2),
        mesh=mesh,
        in_specs=(
            P(("groups", "dom"), None),
            P(("groups", "dom"), None),
            P(),
            P(),
            P(("groups", "dom"), None),
            P(("groups", "dom")),
            P(("groups", "dom"), None, None),
            P(("groups", "dom"), None),
            P(("groups", "dom"), None),
            P(("groups", "dom"), None),
            P(("groups", "dom"), None, None),
        ),
        out_specs=(
            P(("groups", "dom"), None),
            P(("groups", "dom"), None),
            P(("groups", "dom"), None),
        ),
        check_vma=False,
    )
```

```python
import functools

import jax
import jax.numpy as jnp
from jax import lax
from jax.experimental import pallas as pl
from jax.experimental.pallas import tpu as pltpu
from jax.sharding import PartitionSpec as P

MESH = pl.DeviceIdType.MESH
F32 = jnp.float32
BF16 = jnp.bfloat16
PLANE = 4
LANES = 128
PER_PEER = 16


def iota(shape, dim):
    return lax.broadcasted_iota(jnp.int32, shape, dim)


def dot(a, b):
    return jnp.dot(a, b, preferred_element_type=F32)


def dot_nt(a, b):
    return lax.dot_general(a, b, (((1,), (1,)), ((), ())), preferred_element_type=F32)


def dot_tn(a, b):
    return lax.dot_general(a, b, (((0,), (0,)), ((), ())), preferred_element_type=F32)


def step_kernel(
    n, subs, ahead, factor,
    index_ref, hist_hbm, scale_hbm, send_hbm, count_hbm, nb_hbm, f_hbm, mask_hbm, ws_hbm, wn_hbm, ct_hbm,
    gx_ref, gs_ref, gn_ref,
    hist_ref, scale_ref, send_ref, count_ref, nb_ref, f_ref, mask_ref, ws_ref, wn_ref, ct_ref, load_sem,
    out_rows, got_rows, rows_send, rows_recv,
    adj, agg_ref, grad, g_out, g_in, g_send, g_recv,
    f_out, f_in, f_send, f_recv, a_out, a_in, a_send, a_recv,
    part, right_out, right_in, left_out, left_in, right_send, right_recv, left_send, left_recv,
    swap_out, swap_in, swap_send, swap_recv,
):
    me = lax.axis_index("dom")
    core = me % 2
    x = (me // 2) % 2
    z = me // PLANE
    planes = n // PLANE
    rows, width = f_hbm.shape
    tiles, block, _ = mask_hbm.shape
    refs = nb_ref.shape[0]
    cap = send_ref.shape[1]
    hist = hist_ref.shape[0]
    segs = PER_PEER // cap
    seg = width // segs
    wide = n * PER_PEER
    slots = n * cap
    half = width // 2
    sub = half // subs
    units = 2 * subs
    rblk = width // (2 * planes)

    loads = []
    for k, (src, dst) in enumerate(((hist_hbm, hist_ref), (scale_hbm, scale_ref), (send_hbm, send_ref), (count_hbm, count_ref), (nb_hbm, nb_ref), (f_hbm, f_ref), (mask_hbm, mask_ref), (ws_hbm, ws_ref), (wn_hbm, wn_ref), (ct_hbm, ct_ref))):
        load = pltpu.make_async_copy(src, dst, load_sem.at[k])
        loads.append(load)
    for load in loads[:6]:
        load.start()

    barrier = pltpu.get_barrier_semaphore()

    def greet(k, carry):
        pl.semaphore_signal(barrier, inc=1, device_id={"dom": (me + k) % n}, device_id_type=MESH)
        return carry

    lax.fori_loop(1, n, greet, 0)

    for load in loads[:5]:
        load.wait()
    for load in loads[6:]:
        load.start()

    sent = send_ref[0]
    expand = jnp.where((iota((wide, n), 0) // PER_PEER) == iota((wide, n), 1), 1.0, 0.0).astype(BF16)
    low = (sent % 256).astype(F32).astype(BF16)
    high = (sent // 256).astype(F32).astype(BF16)
    spread = dot_nt(expand, low) + 256.0 * dot_nt(expand, high)
    pick = jnp.where(iota((wide, cap), 1) == iota((wide, cap), 0) % cap, spread, 0.0)
    pick = jnp.sum(pick, axis=1, keepdims=True).astype(jnp.int32)
    hot = jnp.where(iota((wide, hist), 1) == pick, scale_ref[...].astype(F32).reshape(1, hist), 0.0).astype(BF16)
    seg_of = (iota((wide, 1), 0) // cap) % segs
    packed = jnp.zeros((wide, seg), F32)
    for j in range(segs):
        packed += dot(hot * (seg_of == j).astype(BF16), hist_ref[:, j * seg:(j + 1) * seg])
    out_rows[...] = packed.astype(BF16).reshape(n, PER_PEER, seg)

    pl.semaphore_wait(barrier, n - 1)

    def row_copy(k, source, target):
        return pltpu.make_async_remote_copy(
            src_ref=out_rows.at[target], dst_ref=got_rows.at[source],
            send_sem=rows_send.at[k], recv_sem=rows_recv.at[k],
            device_id={"dom": target}, device_id_type=MESH)

    def send_rows(k, carry):
        row_copy(k, me, (me + k) % n).start()
        return carry

    lax.fori_loop(1, n, send_rows, 0)
    got_rows[pl.ds(me, 1)] = out_rows[pl.ds(me, 1)]

    sibling = me + 1 - 2 * core
    across = me + 2 - 4 * x
    diagonal = sibling + 2 - 4 * x

    def remote(src, dst, send, recv, target):
        return pltpu.make_async_remote_copy(
            src_ref=src, dst_ref=dst, send_sem=send, recv_sem=recv,
            device_id={"dom": target}, device_id_type=MESH)

    def factor_copies(out, into, send, recv):
        return (
            remote(out.at[:, 1 - x], into.at[1], send.at[1], recv.at[1], across),
            remote(out.at[:, x], into.at[0], send.at[0], recv.at[0], sibling),
            remote(into.at[1], into.at[2], send.at[2], recv.at[2], sibling),
        )

    loads[5].wait()
    for j in range(planes):
        f_out[j] = f_ref[:, j * 2 * rblk:(j + 1) * 2 * rblk].T.reshape(2, rblk, rows)
    f_copies = factor_copies(f_out, f_in, f_send, f_recv)
    f_copies[0].start()
    f_copies[1].start()

    loads[6].wait()
    blocks = rows // block
    degree = []
    for b in range(blocks):
        edges = jnp.zeros((block, 1), F32)
        for e in range(blocks):
            total = jnp.zeros((block, block), jnp.int32)
            for t in range(tiles):
                here = (index_ref[0, t] == b).astype(jnp.int32) * (index_ref[1, t] == e).astype(jnp.int32)
                total += here * mask_ref[t]
            total = total.astype(F32)
            edges += jnp.sum(total, axis=1, keepdims=True)
            adj[b * block:(b + 1) * block, e * block:(e + 1) * block] = total.astype(BF16)
        degree.append(edges)
    degree = jnp.concatenate(degree, axis=0)
    filled = jnp.broadcast_to(count_ref[...], (8, n)).astype(F32).astype(BF16)
    owner = jnp.where(iota((slots, n), 0) // cap == iota((slots, n), 1), 1.0, 0.0).astype(BF16)
    filled = dot_nt(owner, filled)[:, 0:1]
    live = jnp.where((iota((slots, 1), 0) % cap).astype(F32) < filled, 1.0, 0.0)
    count = jnp.zeros((slots, rows), F32)
    for k in range(refs):
        count += jnp.where(nb_ref[k:k + 1, :] == iota((slots, rows), 0), live, 0.0)
    count = count.astype(BF16)
    degree += dot_tn(count, jnp.ones((slots, LANES), BF16))[:, 0:1]
    ws_ready, wn_ready, ct_ready = loads[7:]
    slot_of = (iota((slots, wide), 1) // PER_PEER) * cap + iota((slots, wide), 1) % cap
    same = slot_of == iota((slots, wide), 0)
    spread_seg = (iota((slots, wide), 1) // cap) % segs
    spreads = []
    for j in range(segs):
        e_j = jnp.where(same & (spread_seg == j), 1.0, 0.0).astype(BF16)
        spreads.append(dot_tn(count, e_j).astype(BF16))
    ws_ready.wait()
    wn_ready.wait()
    ct_ready.wait()

    def got(k, carry):
        row_copy(k, (me + n - k) % n, (me + k) % n).wait_recv()
        return carry

    lax.fori_loop(1, n, got, 0)
    rows_in = got_rows[...].reshape(wide, seg)
    for j in range(segs):
        columns = slice(j * seg, (j + 1) * seg)
        total = dot(adj[...], f_ref[:, columns]) + dot(spreads[j], rows_in)
        agg_ref[:, columns] = (total / degree).astype(BF16)

    f_copies[0].wait_recv()
    f_copies[2].start()

    for j in range(planes):
        a_out[j] = agg_ref[:, j * 2 * rblk:(j + 1) * 2 * rblk].T.reshape(2, rblk, rows)
    a_copies = factor_copies(a_out, a_in, a_send, a_recv)

    def g_copies(s):
        return (
            remote(g_out.at[core, s], g_in.at[1, s], g_send.at[1, s], g_recv.at[1, s], across),
            remote(g_out.at[1 - core, s], g_in.at[2, s], g_send.at[2, s], g_recv.at[2, s], diagonal),
            remote(g_out.at[1 - core, s], g_in.at[0, s], g_send.at[0, s], g_recv.at[0, s], sibling),
        )

    for s in range(subs):
        for h in range(2):
            columns = slice(h * half + s * sub, h * half + (s + 1) * sub)
            pre = dot(f_ref[...], ws_ref[:, columns]) + dot(agg_ref[...], wn_ref[:, columns])
            sigma = jax.nn.sigmoid(pre)
            value = (ct_ref[:, columns].astype(F32) * sigma * (1.0 + pre * (1.0 - sigma))).astype(BF16)
            g_out[h, s] = value
            grad[:, columns] = value
        if s < ahead:
            for copy in g_copies(s):
                copy.start()

    back = (dot_nt(grad[...], wn_ref[...]) / degree).astype(BF16)
    gx_ref[...] = (dot_nt(grad[...], ws_ref[...]) + dot_tn(adj[...], back)).astype(BF16)

    last = planes - 1

    def right(u, k):
        return remote(right_out.at[u, k], right_in.at[u, k], right_send.at[u, k], right_recv.at[u, k], (me + PLANE) % n)

    def left(u, k):
        return remote(left_out.at[u, k], left_in.at[u, k], left_send.at[u, k], left_recv.at[u, k], (me + n - PLANE) % n)

    def along(u, first, copy, out, into, order, beyond):
        for k in order:
            @pl.when(beyond(k))
            def _():
                @pl.when(first)
                def _():
                    out[u, k] = part[u, k].astype(BF16)

                @pl.when(jnp.logical_not(first))
                def _():
                    copy(u, k).wait_recv()
                    out[u, k] = (part[u, k] + into[u, k].astype(F32)).astype(BF16)

                copy(u, k).start()

            @pl.when((z == k) & jnp.logical_not(first))
            def _():
                copy(u, k).wait_recv()
                part[u, k] += into[u, k].astype(F32)

    for t in range(units + last):
        if t < units:
            s, m = t % subs, t // subs
            if m == 0:
                for copy in g_copies(s):
                    copy.wait_recv()
                if s + ahead < subs:
                    for copy in g_copies(s + ahead):
                        copy.start()
                elif s + ahead == subs:
                    a_copies[0].start()
                    a_copies[1].start()
            if t == 0:
                f_copies[1].wait_recv()
                f_copies[2].wait_recv()
            if t == subs:
                a_copies[0].wait_recv()
                a_copies[2].start()
                a_copies[1].wait_recv()
                a_copies[2].wait_recv()
            out, into = ((f_out, f_in), (a_out, a_in))[m]
            total = dot(out[:, x].reshape(planes * rblk, rows), g_out[core, s])
            for k in range(3):
                total += dot(into[k].reshape(planes * rblk, rows), g_in[k, s])
            part[t] = total.reshape(planes, rblk, sub)

        @pl.when((t - z >= 0) & (t - z < units))
        def _():
            along(t - z, z == 0, right, right_out, right_in, range(last, 0, -1), lambda k: k > z)

        away = t - (last - z)

        @pl.when((away >= 0) & (away < units))
        def _():
            along(away, z == last, left, left_out, left_in, range(last), lambda k: k < z)

    mine = rblk // 2
    for u in range(units):
        swap_out[u] = part[u, z, pl.ds(pl.multiple_of((1 - core) * mine, mine), mine)] * factor
        remote(swap_out.at[u], swap_in.at[u], swap_send.at[u], swap_recv.at[u], sibling).start()
    for u in range(units):
        s, m = u % subs, u // subs
        out = (gs_ref, gn_ref)[m]
        out[:, pl.ds(pl.multiple_of(core * half + s * sub, LANES), sub)] = (
            part[u, z, pl.ds(pl.multiple_of(core * mine, mine), mine)] * factor)
    for u in range(units):
        s, m = u % subs, u // subs
        out = (gs_ref, gn_ref)[m]
        remote(swap_out.at[u], swap_in.at[u], swap_send.at[u], swap_recv.at[u], sibling).wait()
        out[:, pl.ds(pl.multiple_of((1 - core) * half + s * sub, LANES), sub)] = swap_in[u]

    def left_rows(k, carry):
        row_copy(k, me, (me + k) % n).wait_send()
        return carry

    lax.fori_loop(1, n, left_rows, 0)
    for copy in (*f_copies, *a_copies):
        copy.wait_send()
    for s in range(subs):
        for copy in g_copies(s):
            copy.wait_send()
    for u in range(units):
        for k in range(planes):
            @pl.when(k > z)
            def _():
                right(u, k).wait_send()

            @pl.when(k < z)
            def _():
                left(u, k).wait_send()


def fused(
    subs, ahead, features, cotangent, w_self, w_neigh, history, hist_scale, send_rows, recv_counts, neighbours, tile_index, tile_mask
):
    n = lax.axis_size("dom")
    rows, width = features.shape
    planes = n // PLANE
    cap = send_rows.shape[2]
    seg = width * cap // PER_PEER
    sub = width // 2 // subs
    units = 2 * subs
    rblk = width // (2 * planes)
    factor = float(n * rows) ** (-0.5)
    vmem = pl.BlockSpec(memory_space=pltpu.VMEM)
    smem = pl.BlockSpec(memory_space=pltpu.SMEM)
    far = pl.BlockSpec(memory_space=pltpu.HBM)
    dma = pltpu.SemaphoreType.DMA
    V = pltpu.VMEM
    line = (units, planes, rblk, sub)
    scratch = [
        V(history.shape, BF16), V(hist_scale.shape, BF16), V((1, cap, n), jnp.int32), V(recv_counts.shape, jnp.int32),
        V(neighbours.shape[::-1], jnp.int32),
        V(features.shape, BF16), V(tile_mask.shape, jnp.int32), V(w_self.shape, BF16), V(w_neigh.shape, BF16),
        V(cotangent.shape, BF16), dma((10,)),
        V((n, PER_PEER, seg), BF16), V((n, PER_PEER, seg), BF16), dma((n,)), dma((n,)),
        V((rows, rows), BF16), V((rows, width), BF16), V((rows, width), BF16),
        V((2, subs, rows, sub), BF16), V((3, subs, rows, sub), BF16), dma((3, subs)), dma((3, subs)),
        V((planes, 2, rblk, rows), BF16), V((3, planes, rblk, rows), BF16), dma((3,)), dma((3,)),
        V((planes, 2, rblk, rows), BF16), V((3, planes, rblk, rows), BF16), dma((3,)), dma((3,)),
        V(line, F32), V(line, BF16), V(line, BF16), V(line, BF16), V(line, BF16),
        dma(line[:2]), dma(line[:2]), dma(line[:2]), dma(line[:2]),
        V((units, rblk // 2, sub), F32), V((units, rblk // 2, sub), F32), dma((units,)), dma((units,)),
    ]
    return pl.pallas_call(
        functools.partial(step_kernel, n, subs, ahead, factor),
        out_shape=(
            jax.ShapeDtypeStruct((rows, width), BF16),
            jax.ShapeDtypeStruct((width // n, width), F32),
            jax.ShapeDtypeStruct((width // n, width), F32),
        ),
        in_specs=[smem] + [far] * 10,
        out_specs=(vmem, vmem, vmem),
        scratch_shapes=scratch,
        compiler_params=pltpu.CompilerParams(
            collective_id=0, has_side_effects=True, vmem_limit_bytes=62 * 1024 * 1024),
    )(tile_index.T, history, hist_scale, send_rows.transpose(0, 2, 1), recv_counts, neighbours.T, features,
      tile_mask, w_self, w_neigh, cotangent)


def tiles_forward(inputs, tile_index, masks, block_size):
    row_total, feature_width = inputs.shape
    tile_count = masks.shape[0]
    local_sum = jnp.zeros((row_total, feature_width), jnp.float32)
    edges = jnp.zeros((row_total,), jnp.float32)
    for tile_number in range(tile_count):
        row_block = tile_index[tile_number, 0] * block_size
        col_block = tile_index[tile_number, 1] * block_size
        block = lax.dynamic_slice_in_dim(inputs, col_block, block_size, 0)
        product = jnp.dot(masks[tile_number], block, preferred_element_type=jnp.float32)
        older = lax.dynamic_slice_in_dim(local_sum, row_block, block_size, 0)
        local_sum = lax.dynamic_update_slice_in_dim(local_sum, older + product, row_block, 0)
        older_edges = lax.dynamic_slice_in_dim(edges, row_block, block_size, 0)
        edges = lax.dynamic_update_slice_in_dim(
            edges,
            older_edges + jnp.sum(masks[tile_number].astype(jnp.float32), axis=1),
            row_block,
            0,
        )
    return (local_sum, edges)


def tiles_backward(grad_rows, back_agg, tile_index, masks, block_size):
    tile_count = masks.shape[0]
    contract_rows = (((0,), (0,)), ((), ()))
    for tile_number in range(tile_count):
        row_block = tile_index[tile_number, 0] * block_size
        col_block = tile_index[tile_number, 1] * block_size
        block = lax.dynamic_slice_in_dim(back_agg, row_block, block_size, 0)
        product = lax.dot_general(
            masks[tile_number], block, contract_rows, preferred_element_type=jnp.float32
        )
        older = lax.dynamic_slice_in_dim(grad_rows, col_block, block_size, 0)
        grad_rows = lax.dynamic_update_slice_in_dim(grad_rows, older + product, col_block, 0)
    return grad_rows


def plain_shards(
    features,
    cotangent,
    w_self,
    w_neigh,
    history,
    hist_scale,
    send_rows,
    recv_counts,
    neighbours,
    tile_index,
    tile_mask,
):
    row_total, feature_width = features.shape
    peer_count = lax.axis_size("dom")
    slot_cap = send_rows.shape[2]
    block_size = tile_mask.shape[1]
    picked = send_rows[0]
    out_rows = history[picked]
    out_scale = hist_scale[picked]
    got_rows, got_scale = (
        lax.all_to_all(out_rows, "dom", split_axis=0, concat_axis=0, tiled=True),
        lax.all_to_all(out_scale, "dom", split_axis=0, concat_axis=0, tiled=True),
    )
    slot_total = peer_count * slot_cap
    got_rows = got_rows.reshape(slot_total, feature_width)
    got_scale = got_scale.reshape(slot_total).astype(jnp.float32)
    masks = tile_mask.astype(jnp.bfloat16)
    local_sum, edges = tiles_forward(features, tile_index, masks, block_size)
    counts = recv_counts[0]
    owner = neighbours // slot_cap
    position = neighbours % slot_cap
    live = (position < counts[owner]).astype(jnp.float32)
    weight = live * got_scale[neighbours]
    row_ids = jnp.broadcast_to(jnp.arange(row_total, dtype=jnp.int32)[:, None], neighbours.shape)
    slot_weight = (
        jnp.zeros((row_total, slot_total), jnp.float32).at[row_ids, neighbours].add(weight)
    )
    remote_sum = jnp.dot(slot_weight, got_rows.astype(jnp.float32), precision=lax.Precision.HIGHEST)
    degree = edges + jnp.sum(live, axis=1)
    agg = ((local_sum + remote_sum) / degree[:, None]).astype(jnp.bfloat16)
    pre = jnp.dot(features, w_self, preferred_element_type=jnp.float32) + jnp.dot(
        agg, w_neigh, preferred_element_type=jnp.float32
    )
    sigma = jax.nn.sigmoid(pre)
    grad_pre = (cotangent.astype(jnp.float32) * sigma * (1.0 + pre * (1.0 - sigma))).astype(
        jnp.bfloat16
    )
    factor = float(peer_count * row_total) ** (-0.5)
    contract_rows = (((0,), (0,)), ((), ()))
    contract_cols = (((1,), (1,)), ((), ()))
    columns = features
    grad_self = lax.psum_scatter(
        lax.dot_general(columns, grad_pre, contract_rows, preferred_element_type=jnp.float32)
        * factor,
        "dom",
        scatter_dimension=0,
        tiled=True,
    )
    columns = agg
    grad_neigh = lax.psum_scatter(
        lax.dot_general(columns, grad_pre, contract_rows, preferred_element_type=jnp.float32)
        * factor,
        "dom",
        scatter_dimension=0,
        tiled=True,
    )
    back = lax.dot_general(grad_pre, w_neigh, contract_cols, preferred_element_type=jnp.float32)
    back_agg = (back / degree[:, None]).astype(jnp.bfloat16)
    grad_rows = lax.dot_general(grad_pre, w_self, contract_cols, preferred_element_type=jnp.float32)
    grad_rows = tiles_backward(grad_rows, back_agg, tile_index, masks, block_size)
    return (grad_rows.astype(jnp.bfloat16), grad_self, grad_neigh)


def shards(subs, ahead, *args):
    features, send_rows, tile_mask = args[0], args[6], args[10]
    n = lax.axis_size("dom")
    width = features.shape[1]
    cap = send_rows.shape[2]
    whole_blocks = n % PLANE == 0 and (2 * width) % (n * LANES) == 0
    if whole_blocks and PER_PEER % cap == 0 and features.shape[0] % LANES == 0:
        return fused(subs, ahead, *args)
    return plain_shards(*args)


def solution(mesh):
    return jax.shard_map(
        functools.partial(shards, 2, 2),
        mesh=mesh,
        in_specs=(
            P(("groups", "dom"), None),
            P(("groups", "dom"), None),
            P(),
            P(),
            P(("groups", "dom"), None),
            P(("groups", "dom")),
            P(("groups", "dom"), None, None),
            P(("groups", "dom"), None),
            P(("groups", "dom"), None),
            P(("groups", "dom"), None),
            P(("groups", "dom"), None, None),
        ),
        out_specs=(
            P(("groups", "dom"), None),
            P(("groups", "dom"), None),
            P(("groups", "dom"), None),
        ),
        check_vma=False,
    )
```
